256 devices in a mesh: kz: 16 (over z, x_lo), en: 16 (over x_hi, y, core).
Axes of the slice: x: 4 (x_hi: 2, x_lo: 2; x = x_hi * 2 + x_lo), y: 4, z: 8, core: 2. Of those that a mesh axis runs over, the one named last changes fastest.
Arguments:
- green_real: bfloat16 [16, 384, 128, 128], P('kz', 'en'), may hold values from -6 to 6
- green_imag: bfloat16 [16, 384, 128, 128], P('kz', 'en'), may hold values from -6 to 6
- coupling: bfloat16 [2, 4, 16, 128, 128], P(None, None, 'kz'), may hold values from -0.5 to 0.5
- strengths: float32 [2, 4, 8], replicated, may hold values from 0.1 to 1
- offsets: int32 [2, 8], replicated, may hold values from -4 to 4, as said below
Outputs:
- dressed_real: bfloat16 [16, 384, 128, 128], P('kz', 'en')
- dressed_imag: bfloat16 [16, 384, 128, 128], P('kz', 'en')
The draws below stay inside these ranges and needn't reach their ends.
Inputs may be any that keep to these rules, and one draw needn't show every extreme that they name: Each row of offsets holds each of -4 to -1 and 1 to 4 exactly once.
All inputs are finite; a program needn't handle non-finite values.
Results may differ from the reference program's by a relative error of at most 0.007.
Values may be sent and summed in bfloat16 or wider, within the bound.
No kernel may reach another device: no remote copies, remote signals or barrier semaphores. Data moves between devices by JAX's collectives and lax.ppermute only.
A program may use at most 128 MiB of HBM per device.

```python
import math
import jax
import jax.numpy as jnp
from jax import lax

NO = 128
REACH = 4
HOPS = 2
BRANCHES = 4
OFFS = 8
NK = 16
NE = 384


def draw_offsets(key, part):
    base_list = jnp.concatenate([jnp.arange(-REACH, 0), jnp.arange(1, REACH + 1)]).astype(jnp.int32)
    key_list = jax.random.split(key, HOPS)
    rows_list = [jax.random.permutation(key_list[hop_index], base_list) for hop_index in range(HOPS)]
    return jnp.stack(rows_list).astype(jnp.int32)


def steps_of(key, dims, shards, least, largest):
    gain, own = 1.0, jax.random.fold_in(key, 6)
    for dim, parts in shards:
        draws = jnp.exp(jax.random.uniform(jax.random.fold_in(own, dim), (parts,), jnp.float32, least / len(shards), largest / len(shards)))
        gain = gain * jnp.repeat(draws, dims[dim] // parts).reshape([-1 if axis == dim else 1 for axis in range(len(dims))])
    return gain


def noise(own_key, extent, spread, bound, pieces=(), dtype=jnp.bfloat16):
    factor_of = steps_of(own_key, extent, pieces, -0.22, 0.18) if pieces else 1.0
    result = jax.random.normal(own_key, extent, jnp.float32) * spread * factor_of
    return jnp.minimum(jnp.maximum(result, -bound), bound).astype(dtype)


def setup_inputs(seed: int = 0) -> dict:
    splits = jax.random.split(jax.random.key(seed), 6)
    green_real = noise(splits[0], (NK, NE, NO, NO), 1.0, 6.0, ((0, 16), (1, 16)))
    green_imag = noise(splits[1], (NK, NE, NO, NO), 1.0, 6.0, ((0, 16), (1, 16)))
    coupling = noise(splits[2], (HOPS, BRANCHES, NK, NO, NO), NO ** -0.5, 0.5, ((2, 16),))
    strengths = jnp.clip(jnp.exp(jax.random.uniform(splits[3], (HOPS, BRANCHES, OFFS), jnp.float32, math.log(0.1), math.log(1.0))), 0.1, 1.0)
    offsets = draw_offsets(jax.random.fold_in(splits[5], 71), 0)
    return dict(green_real=green_real, green_imag=green_imag, coupling=coupling, strengths=strengths, offsets=offsets)


def reference(green_real, green_imag, coupling, strengths, offsets):
    stacked = jnp.stack([green_real, green_imag], axis=1)
    levels = jnp.arange(-REACH, REACH + 1).astype(jnp.int32)
    match_table = (offsets[:, None, :, None] == levels[None, None, None, :]).astype(jnp.float32)
    weights_table = jnp.sum(strengths[:, :, :, None] * match_table, axis=2)

    def per_momentum(momentum):
        own_block = lax.dynamic_index_in_dim(stacked, momentum, 0, keepdims=False).astype(jnp.float32)
        self_energy = jnp.zeros(own_block.shape, jnp.float32)
        for hop_index in range(HOPS):
            source = lax.dynamic_index_in_dim(stacked, ((momentum - hop_index - 1) % NK).astype(jnp.int32), 0, keepdims=False).astype(jnp.float32)
            padded = jnp.pad(source, ((0, 0), (REACH, REACH), (0, 0), (0, 0)))
            for branch_index in range(BRANCHES):
                summed_block = jnp.zeros(own_block.shape, jnp.float32)
                for step_index in range(2 * REACH + 1):
                    energy_shift = step_index - REACH
                    if energy_shift == 0:
                        continue
                    summed_block = summed_block + weights_table[hop_index, branch_index, step_index] * padded[:, REACH - energy_shift:REACH - energy_shift + NE]
                summed_block = lax.optimization_barrier(summed_block.astype(jnp.bfloat16)).astype(jnp.float32)
                matrix = lax.dynamic_index_in_dim(coupling[hop_index, branch_index], momentum, 0, keepdims=False).astype(jnp.float32)
                left_prod = jnp.einsum("ab,xebc->xeac", matrix, summed_block)
                left_prod = lax.optimization_barrier(left_prod.astype(jnp.bfloat16)).astype(jnp.float32)
                self_energy = self_energy + jnp.einsum("xeab,cb->xeac", left_prod, matrix)
        self_energy = lax.optimization_barrier(self_energy.astype(jnp.bfloat16)).astype(jnp.float32)
        real_part = own_block[0]
        imag_part = own_block[1]
        self_real = self_energy[0]
        self_imag = self_energy[1]
        prod_real = jnp.einsum("eab,ebc->eac", real_part, self_real) - jnp.einsum("eab,ebc->eac", imag_part, self_imag)
        prod_imag = jnp.einsum("eab,ebc->eac", real_part, self_imag) + jnp.einsum("eab,ebc->eac", imag_part, self_real)
        prod_real = lax.optimization_barrier(prod_real.astype(jnp.bfloat16)).astype(jnp.float32)
        prod_imag = lax.optimization_barrier(prod_imag.astype(jnp.bfloat16)).astype(jnp.float32)
        back_real = jnp.einsum("eab,ebc->eac", prod_real, real_part) - jnp.einsum("eab,ebc->eac", prod_imag, imag_part)
        back_imag = jnp.einsum("eab,ebc->eac", prod_real, imag_part) + jnp.einsum("eab,ebc->eac", prod_imag, real_part)
        dressed_real = (real_part + back_real / NO).astype(jnp.bfloat16)
        dressed_imag = (imag_part + back_imag / NO).astype(jnp.bfloat16)
        return jnp.stack([dressed_real, dressed_imag])

    results = lax.map(per_momentum, jnp.arange(NK).astype(jnp.int32))
    return (results[:, 0], results[:, 1])
```

```python
import functools

import jax
import jax.numpy as jnp
from jax import lax
from jax.experimental import pallas as pl
from jax.experimental.pallas import tpu as pltpu
from jax.sharding import PartitionSpec as P

REACH = 4
HOPS = 2
BRANCHES = 4
WINDOW = 2 * REACH
VMEM_LIMIT = 40 * 2**20

F32 = jnp.float32
BF16 = jnp.bfloat16
dot = functools.partial(jnp.dot, preferred_element_type=F32)
WHOLE = pl.BlockSpec(memory_space=pltpu.VMEM)
SCALARS = pl.BlockSpec(memory_space=pltpu.SMEM)
UNTOUCHED = pl.BlockSpec(memory_space=pl.ANY)


def prepare_kernel(offsets_ref, strengths_ref, coupling_ref, weights_ref, joined_ref):
    no = coupling_ref.shape[-1]
    for s in range(HOPS):
        for n in range(BRANCHES):
            matrix = coupling_ref[s, n, 0]
            joined_ref[s, :, n * no : (n + 1) * no] = matrix
            turned = matrix.astype(F32).T
            for i in range(WINDOW):
                w = offsets_ref[s, i]
                j = jnp.where(w > 0, REACH - w, REACH - 1 - w)
                rows = pl.ds(pl.multiple_of(j * no, no), no)
                weights_ref[s, rows, n * no : (n + 1) * no] = (strengths_ref[s, n, i] * turned).astype(BF16)


def prepare(coupling, strengths, offsets):
    no = coupling.shape[-1]
    return pl.pallas_call(
        prepare_kernel,
        out_shape=(
            jax.ShapeDtypeStruct((HOPS, WINDOW * no, BRANCHES * no), BF16),
            jax.ShapeDtypeStruct((HOPS, no, BRANCHES * no), BF16),
        ),
        in_specs=[SCALARS, SCALARS, WHOLE],
        out_specs=(WHOLE, WHOLE),
        compiler_params=pltpu.CompilerParams(vmem_limit_bytes=VMEM_LIMIT),
        cost_estimate=pl.CostEstimate(flops=10**6, bytes_accessed=3 * 10**6, transcendentals=0),
        name="prepare",
    )(offsets, strengths, coupling)


def hop_terms(s, tiles, first, weights_ref, joined_ref):
    no = joined_ref.shape[1]
    energy = lambda t: tiles[first + t // REACH][t % REACH]
    rows = []
    for i in range(REACH):
        rows.append(jnp.concatenate([energy(i + j + (j >= REACH)) for j in range(WINDOW)], axis=1))
    right = dot(jnp.concatenate(rows, axis=0), weights_ref[s]).astype(BF16)
    terms = []
    for i in range(REACH):
        stacked = []
        for n in range(BRANCHES):
            block = right[i * 2 * no : (i + 1) * 2 * no, n * no : (n + 1) * no]
            stacked.append(jnp.concatenate([block[:no], block[no:]], axis=1))
        terms.append(dot(joined_ref[s], jnp.concatenate(stacked, axis=0)))
    return terms


def far_kernel(count, *refs):
    tiles, (weights_ref, joined_ref, out_ref) = refs[: count + 2], refs[count + 2 :]
    for c in range(count):
        for i, term in enumerate(hop_terms(1, tiles, c, weights_ref, joined_ref)):
            out_ref[c * REACH + i] = term


def far_part(tiles, weights, joined):
    count = len(tiles) - 2
    no = joined.shape[1]
    return pl.pallas_call(
        functools.partial(far_kernel, count),
        out_shape=jax.ShapeDtypeStruct((count * REACH, no, 2 * no), F32),
        in_specs=[WHOLE] * (count + 4),
        out_specs=WHOLE,
        compiler_params=pltpu.CompilerParams(vmem_limit_bytes=VMEM_LIMIT),
        cost_estimate=pl.CostEstimate(flops=count * 2 * 10**9, bytes_accessed=2 * 10**6, transcendentals=0),
        name="far_part",
    )(*tiles, weights, joined)


def crossed(real, imag):
    return jnp.concatenate(
        [jnp.concatenate([real, imag], axis=1), jnp.concatenate([-imag, real], axis=1)], axis=0
    )


def near_kernel(count, *refs):
    tiles, refs = refs[: count + 2], refs[count + 2 :]
    weights_ref, joined_ref, real_ref, imag_ref = refs[:4]
    parts, refs = refs[4 : 4 + count], refs[4 + count :]
    out_real_ref, out_imag_ref = refs[-2:]
    no = joined_ref.shape[1]
    for c in range(count):
        for i, term in enumerate(hop_terms(0, tiles, c, weights_ref, joined_ref)):
            e = c * REACH + i
            sigma = (term + parts[c][i]).astype(BF16)
            real, imag = real_ref[0, e], imag_ref[0, e]
            prod = dot(jnp.concatenate([real, imag], axis=1), crossed(sigma[:, :no], sigma[:, no:])).astype(BF16)
            back = dot(prod, crossed(real, imag)) / no
            out_real_ref[0, e] = (real.astype(F32) + back[:, :no]).astype(BF16)
            out_imag_ref[0, e] = (imag.astype(F32) + back[:, no:]).astype(BF16)


def near_part(tiles, weights, joined, green, parts, start, so_far):
    count = len(tiles) - 2
    no = joined.shape[1]
    size = count * REACH
    own = pl.BlockSpec((1, size, no, no), lambda g: (0, start // size, 0, 0))
    shape = jax.ShapeDtypeStruct(green[0].shape, BF16)
    inputs = [*tiles, weights, joined, *green, *parts]
    in_specs = [WHOLE] * (count + 4) + [own] * 2 + [WHOLE] * count
    aliases = {}
    if so_far is not None:
        aliases = {len(inputs): 0, len(inputs) + 1: 1}
        inputs += so_far
        in_specs += [UNTOUCHED] * 2
    return pl.pallas_call(
        functools.partial(near_kernel, count),
        grid=(1,),
        out_shape=(shape, shape),
        in_specs=in_specs,
        out_specs=(own, own),
        input_output_aliases=aliases,
        compiler_params=pltpu.CompilerParams(vmem_limit_bytes=VMEM_LIMIT),
        cost_estimate=pl.CostEstimate(flops=count * 25 * 10**8, bytes_accessed=4 * 10**6, transcendentals=0),
        name="near_part",
    )(*inputs)


def shards(green_real, green_imag, coupling, strengths, offsets):
    energies = green_real.shape[1]
    momenta = lax.axis_size("kz")
    lanes = lax.axis_size("en")
    chunks = energies // REACH
    two_on = [(i, (i + 2) % momenta) for i in range(momenta)]
    swap = [(i, i ^ 1) for i in range(momenta)]
    up = [(i, i + 1) for i in range(lanes - 1)]
    down = [(i + 1, i) for i in range(lanes - 1)]
    even = lax.axis_index("kz") % 2 == 0

    def own_chunk(c):
        cut = slice(c * REACH, (c + 1) * REACH)
        return jnp.concatenate([green_real[0, cut], green_imag[0, cut]], axis=1)

    order = [0, chunks - 1] + list(range(1, chunks - 1))
    own, far, near = {}, {}, {}
    for c in order:
        own[c] = own_chunk(c)
        far[c] = lax.ppermute(own[c], "kz", two_on)
    weights, joined = prepare(coupling, strengths, offsets)
    for c in order:
        near[c] = lax.ppermute(jnp.where(even, own[c], far[c]), "kz", swap)
    last = chunks - 1
    below = lax.ppermute(jnp.stack([near[last], far[last]]), "en", up)
    above = lax.ppermute(jnp.stack([near[0], far[0]]), "en", down)
    near[-1], far[-1] = below[0], below[1]
    near[chunks], far[chunks] = above[0], above[1]

    out = None
    green = (green_real, green_imag)
    groups = [[c] for c in range(chunks // 2)] + [list(range(chunks // 2, chunks))]
    for group in groups:
        around = range(group[0] - 1, group[-1] + 2)
        parts = [far_part([far[n] for n in (c - 1, c, c + 1)], weights, joined) for c in group]
        out = near_part([near[n] for n in around], weights, joined, green, parts, group[0] * REACH, out)
    return tuple(out)


def solution(mesh):
    in_specs = (
        P("kz", "en", None, None),
        P("kz", "en", None, None),
        P(None, None, "kz", None, None),
        P(),
        P(),
    )
    out_specs = (P("kz", "en", None, None), P("kz", "en", None, None))
    return jax.shard_map(shards, mesh=mesh, in_specs=in_specs, out_specs=out_specs, check_vma=False)
```

```python
import functools

import jax
import jax.numpy as jnp
from jax import lax
from jax.experimental import pallas as pl
from jax.experimental.pallas import tpu as pltpu
from jax.sharding import PartitionSpec as P

REACH = 4
HOPS = 2
BRANCHES = 4
WINDOW = 2 * REACH
AHEAD = 2
VMEM_LIMIT = 40 * 2**20

F32 = jnp.float32
BF16 = jnp.bfloat16
dot = functools.partial(jnp.dot, preferred_element_type=F32)
WHOLE = pl.BlockSpec(memory_space=pltpu.VMEM)
SCALARS = pl.BlockSpec(memory_space=pltpu.SMEM)
UNTOUCHED = pl.BlockSpec(memory_space=pl.ANY)
FREE = pl.CostEstimate(flops=0, bytes_accessed=10**6, transcendentals=0)


def prepare_kernel(offsets_ref, strengths_ref, coupling_ref, *outs):
    no = coupling_ref.shape[-1]
    for s in range(HOPS):
        weights_ref, joined_ref = outs[2 * s : 2 * s + 2]
        for n in range(BRANCHES):
            matrix = coupling_ref[s, n, 0]
            joined_ref[:, n * no : (n + 1) * no] = matrix
            turned = matrix.astype(F32).T
            for i in range(WINDOW):
                w = offsets_ref[s, i]
                j = jnp.where(w > 0, REACH - w, REACH - 1 - w)
                rows = pl.ds(pl.multiple_of(j * no, no), no)
                weights_ref[rows, n * no : (n + 1) * no] = (strengths_ref[s, n, i] * turned).astype(BF16)


def prepare(coupling, strengths, offsets):
    no = coupling.shape[-1]
    outs = pl.pallas_call(
        prepare_kernel,
        out_shape=[
            jax.ShapeDtypeStruct((WINDOW * no, BRANCHES * no), BF16),
            jax.ShapeDtypeStruct((no, BRANCHES * no), BF16),
        ]
        * HOPS,
        in_specs=[SCALARS, SCALARS, WHOLE],
        out_specs=[WHOLE] * (2 * HOPS),
        compiler_params=pltpu.CompilerParams(vmem_limit_bytes=VMEM_LIMIT),
        cost_estimate=FREE,
        name="prepare",
    )(offsets, strengths, coupling)
    return outs[:2], outs[2:]


def hop_terms(odd_ref, tiles, first, weights_ref, joined_ref):
    no = joined_ref.shape[0]

    def energy(t):
        tile = tiles[first + t // REACH]
        if isinstance(tile, tuple):
            return jnp.where(odd_ref[0] > 0, tile[0][t % REACH], tile[1][t % REACH])
        return tile[t % REACH]

    rows = []
    for i in range(REACH):
        rows.append(jnp.concatenate([energy(i + j + (j >= REACH)) for j in range(WINDOW)], axis=1))
    right = dot(jnp.concatenate(rows, axis=0), weights_ref[...]).astype(BF16)
    terms = []
    for i in range(REACH):
        stacked = []
        for n in range(BRANCHES):
            block = right[i * 2 * no : (i + 1) * 2 * no, n * no : (n + 1) * no]
            stacked.append(jnp.concatenate([block[:no], block[no:]], axis=1))
        terms.append(dot(joined_ref[...], jnp.concatenate(stacked, axis=0)))
    return terms


def regroup(layout, refs):
    refs = iter(refs)
    return [(next(refs), next(refs)) if pair else next(refs) for pair in layout]


def flat(tiles):
    layout = tuple(isinstance(tile, tuple) for tile in tiles)
    return layout, [x for tile in tiles for x in (tile if isinstance(tile, tuple) else (tile,))]


def far_kernel(layout, odd_ref, *refs):
    width = len(layout) + sum(layout)
    tiles, (weights_ref, joined_ref, *outs) = regroup(layout, refs[:width]), refs[width:]
    count = len(layout) - 2
    for c in range(count):
        for i, term in enumerate(hop_terms(odd_ref, tiles, c, weights_ref, joined_ref)):
            outs[c][i] = term


def far_part(odd, tiles, weights, joined):
    count = len(tiles) - 2
    layout, tiles = flat(tiles)
    no = joined.shape[0]
    return pl.pallas_call(
        functools.partial(far_kernel, layout),
        out_shape=[jax.ShapeDtypeStruct((REACH, no, 2 * no), F32)] * count,
        in_specs=[SCALARS] + [WHOLE] * (len(tiles) + 2),
        out_specs=[WHOLE] * count,
        compiler_params=pltpu.CompilerParams(vmem_limit_bytes=VMEM_LIMIT),
        cost_estimate=FREE,
        name="far_part",
    )(odd, *tiles, weights, joined)


def crossed(real, imag):
    return jnp.concatenate(
        [jnp.concatenate([real, imag], axis=1), jnp.concatenate([-imag, real], axis=1)], axis=0
    )


def near_kernel(layouts, odd_ref, *refs):
    count = len(layouts[1])
    width, own_width = (len(layout) + sum(layout) for layout in layouts)
    tiles, refs = regroup(layouts[0], refs[:width]), refs[width:]
    owns, refs = regroup(layouts[1], refs[:own_width]), refs[own_width:]
    weights_ref, joined_ref = refs[:2]
    parts = refs[2 : 2 + count]
    out_real_ref, out_imag_ref = refs[-2:]
    no = joined_ref.shape[0]
    for c in range(count):

        @pl.when(pl.program_id(0) == c)
        def _():
            terms = hop_terms(odd_ref, tiles, c, weights_ref, joined_ref)
            sigmas = [(term + parts[c][i]).astype(BF16) for i, term in enumerate(terms)]
            greens = []
            for i in range(REACH):
                own = owns[c]
                green = jnp.where(odd_ref[0] > 0, own[0][i], own[1][i]) if isinstance(own, tuple) else own[i]
                greens.append((green[:no], green[no:]))
            prods = [
                dot(jnp.concatenate(pair, axis=1), crossed(sigma[:, :no], sigma[:, no:])).astype(BF16)
                for pair, sigma in zip(greens, sigmas)
            ]
            backs = [dot(prod, crossed(*pair)) / no for pair, prod in zip(greens, prods)]
            for i, ((real, imag), back) in enumerate(zip(greens, backs)):
                out_real_ref[0, i] = (real.astype(F32) + back[:, :no]).astype(BF16)
                out_imag_ref[0, i] = (imag.astype(F32) + back[:, no:]).astype(BF16)


def near_part(odd, tiles, weights, joined, owns, parts, start, shape, so_far):
    count = len(owns)
    layout, tiles = flat(tiles)
    own_layout, owns = flat(owns)
    no = joined.shape[0]
    block = pl.BlockSpec((1, REACH, no, no), lambda g: (0, start + g, 0, 0))
    shape = jax.ShapeDtypeStruct(shape, BF16)
    inputs = [odd, *tiles, *owns, weights, joined, *parts]
    in_specs = [SCALARS] + [WHOLE] * (len(inputs) - 1)
    aliases = {}
    if so_far is not None:
        aliases = {len(inputs): 0, len(inputs) + 1: 1}
        inputs += so_far
        in_specs += [UNTOUCHED] * 2
    return pl.pallas_call(
        functools.partial(near_kernel, (layout, own_layout)),
        grid=(count,),
        out_shape=(shape, shape),
        in_specs=in_specs,
        out_specs=(block, block),
        input_output_aliases=aliases,
        compiler_params=pltpu.CompilerParams(vmem_limit_bytes=VMEM_LIMIT),
        cost_estimate=FREE,
        name="near_part",
    )(*inputs)


def tied(x, *deps):
    return lax.optimization_barrier((x, *deps))[0] if deps else x


def shards(green_real, green_imag, coupling, strengths, offsets):
    chunks = green_real.shape[1] // REACH
    momenta, lanes = lax.axis_size("kz"), lax.axis_size("en")
    both = ("kz", "en")
    even = lax.axis_index("kz") % 2 == 0
    lane = lax.axis_index("en")
    odd_lane = lane % 2 == 1
    middle = lanes // 2
    at_middle = (lane == middle - 1) | (lane == middle)
    two_on = [(i, (i + 2) % momenta) for i in range(momenta)]
    swap = [(i, i ^ 1) for i in range(momenta)]
    outer = [p for m in range(1, lanes - 1, 2) for p in ((m, m + 1), (m + 1, m))]
    inner = [(i, i ^ 1) for i in range(lanes)]
    outer_turned = [
        (k * lanes + i, (k ^ 1 if {i, j} == {middle - 1, middle} else k) * lanes + j)
        for k in range(momenta)
        for i, j in outer
    ]

    def by_lane(odd, other):
        return jnp.where(odd_lane, odd, other)

    last = chunks - 1
    def cut(c, real, imag):
        energies = slice(c * REACH, (c + 1) * REACH)
        return jnp.concatenate([real[0, energies], imag[0, energies]], axis=1)

    green = (green_real, green_imag)
    own = [by_lane(cut(last, *green), cut(0, *green))]
    far, near = [lax.ppermute(own[0], "kz", two_on)], []
    green = lax.optimization_barrier((*green, own[0]))[:2]
    own.append(by_lane(cut(0, *green), cut(last, *green)))
    own += [cut(c, *green) for c in range(1, last)]
    for i in range(1, chunks):
        if i >= AHEAD:
            own[i] = tied(own[i], far[i - AHEAD])
        far.append(lax.ppermute(own[i], "kz", two_on))
    near_side, far_side = prepare(coupling, strengths, offsets)

    def arranged(sent, outer_halo, inner_halo):
        below, first = (inner_halo, outer_halo), (sent[1], sent[0])
        top, above = (sent[0], sent[1]), (outer_halo, inner_halo)
        return [below, first, *sent[2:], top, above]

    shape = green_real.shape
    odd = odd_lane.astype(jnp.int32).reshape(1)
    out, done = None, (far_side[0],)
    parts, halos, source = {}, {}, []
    far_work = {2: [0], 3: [1], 4: [2], 5: [3, 4, 5]}
    near_work = {4: [0], 5: [1]}
    rest = [2, 3, 4, 5]

    def grouped(sent, side, group):
        sent = sent + [sent[-1]] * (chunks - len(sent))
        return arranged(sent, halos[side, "outer"], halos[side, "inner"])[group[0] : group[-1] + 3]

    def after(tiles, done):
        tiles[-1] = tuple(tied(x, *done) for x in tiles[-1]) if isinstance(tiles[-1], tuple) else tied(tiles[-1], *done)
        return tiles

    for i in range(chunks):
        if i >= 2:
            done += (near[i - 2],)
        if i == 4:
            done += (halos["near", "outer"],)
        far[i] = tied(far[i], *done)
        source.append(jnp.where(even, own[i], far[i]))
        gate = [source[i]]
        if i == 0:
            halos["far", "outer"] = lax.ppermute(far[0], "en", outer)
        near.append(lax.ppermute(source[i], "kz", swap))
        if i == 1:
            halos["far", "inner"] = lax.ppermute(far[1], "en", inner)
        if i == 2:
            edge = tied(jnp.where(at_middle, source[0], near[0]), source[i])
            halos["near", "outer"] = lax.ppermute(edge, both, outer_turned)
            gate.append(edge)
        if i == 3:
            edge = tied(near[1], source[i])
            halos["near", "inner"] = lax.ppermute(edge, "en", inner)
            gate.append(edge)
        done = tuple(gate)
        if i in far_work:
            group = far_work[i]
            part = far_part(odd, after(grouped(far, "far", group), done), *far_side)
            for n, c in enumerate(group):
                parts[c] = part[n]
            done = (part[-1],)
        for c in near_work.get(i, []):
            owns = arranged(own, own[0], own[0])[c + 1 : c + 2]
            tiles = grouped(near, "near", [c])
            tiles[2] = tied(tiles[2], *done)
            out = near_part(odd, tiles, *near_side, owns, [parts[c]], c, shape, out)
            done = (out[0],)
    owns = arranged(own, own[0], own[0])[rest[0] + 1 : rest[-1] + 2]
    out = near_part(
        odd, grouped(near, "near", rest), *near_side, owns, [parts[c] for c in rest], rest[0], shape, out
    )
    return tuple(out)


def solution(mesh):
    in_specs = (
        P("kz", "en", None, None),
        P("kz", "en", None, None),
        P(None, None, "kz", None, None),
        P(),
        P(),
    )
    out_specs = (P("kz", "en", None, None), P("kz", "en", None, None))
    return jax.shard_map(shards, mesh=mesh, in_specs=in_specs, out_specs=out_specs, check_vma=False)
```

```python
import functools

import jax
import jax.numpy as jnp
from jax import lax
from jax.experimental import pallas as pl
from jax.experimental.pallas import tpu as pltpu
from jax.sharding import PartitionSpec as P

REACH = 4
HOPS = 2
BRANCHES = 4
WINDOW = 2 * REACH
AHEAD = 2
VMEM_LIMIT = 40 * 2**20

F32 = jnp.float32
BF16 = jnp.bfloat16
dot = functools.partial(jnp.dot, preferred_element_type=F32)
WHOLE = pl.BlockSpec(memory_space=pltpu.VMEM)
SCALARS = pl.BlockSpec(memory_space=pltpu.SMEM)
UNTOUCHED = pl.BlockSpec(memory_space=pl.ANY)
FREE = pl.CostEstimate(flops=0, bytes_accessed=10**6, transcendentals=0)


def prepare_kernel(offsets_ref, strengths_ref, coupling_ref, *outs):
    no = coupling_ref.shape[-1]
    for s in range(HOPS):
        weights_ref, joined_ref = outs[2 * s : 2 * s + 2]
        for n in range(BRANCHES):
            matrix = coupling_ref[s, n, 0]
            joined_ref[:, n * no : (n + 1) * no] = matrix
            turned = matrix.astype(F32).T
            for i in range(WINDOW):
                w = offsets_ref[s, i]
                j = jnp.where(w > 0, REACH - w, REACH - 1 - w)
                rows = pl.ds(pl.multiple_of(j * no, no), no)
                weights_ref[rows, n * no : (n + 1) * no] = (strengths_ref[s, n, i] * turned).astype(BF16)


def prepare(coupling, strengths, offsets):
    no = coupling.shape[-1]
    outs = pl.pallas_call(
        prepare_kernel,
        out_shape=[
            jax.ShapeDtypeStruct((WINDOW * no, BRANCHES * no), BF16),
            jax.ShapeDtypeStruct((no, BRANCHES * no), BF16),
        ]
        * HOPS,
        in_specs=[SCALARS, SCALARS, WHOLE],
        out_specs=[WHOLE] * (2 * HOPS),
        compiler_params=pltpu.CompilerParams(vmem_limit_bytes=VMEM_LIMIT),
        cost_estimate=FREE,
        name="prepare",
    )(offsets, strengths, coupling)
    return outs[:2], outs[2:]


def hop_terms(odd_ref, tiles, first, weights_ref, joined_ref):
    no = joined_ref.shape[0]

    def energy(t):
        tile = tiles[first + t // REACH]
        if isinstance(tile, tuple):
            return jnp.where(odd_ref[0] > 0, tile[0][t % REACH], tile[1][t % REACH])
        return tile[t % REACH]

    rows = []
    for i in range(REACH):
        rows.append(jnp.concatenate([energy(i + j + (j >= REACH)) for j in range(WINDOW)], axis=1))
    right = dot(jnp.concatenate(rows, axis=0), weights_ref[...]).astype(BF16)
    terms = []
    for i in range(REACH):
        stacked = []
        for n in range(BRANCHES):
            block = right[i * 2 * no : (i + 1) * 2 * no, n * no : (n + 1) * no]
            stacked.append(jnp.concatenate([block[:no], block[no:]], axis=1))
        terms.append(dot(joined_ref[...], jnp.concatenate(stacked, axis=0)))
    return terms


def regroup(layout, refs):
    refs = iter(refs)
    return [(next(refs), next(refs)) if pair else next(refs) for pair in layout]


def flat(tiles):
    layout = tuple(isinstance(tile, tuple) for tile in tiles)
    return layout, [x for tile in tiles for x in (tile if isinstance(tile, tuple) else (tile,))]


def far_kernel(layout, odd_ref, *refs):
    width = len(layout) + sum(layout)
    tiles, (weights_ref, joined_ref, *outs) = regroup(layout, refs[:width]), refs[width:]
    count = len(layout) - 2
    for c in range(count):
        for i, term in enumerate(hop_terms(odd_ref, tiles, c, weights_ref, joined_ref)):
            outs[c][i] = term


def far_part(odd, tiles, weights, joined):
    count = len(tiles) - 2
    layout, tiles = flat(tiles)
    no = joined.shape[0]
    return pl.pallas_call(
        functools.partial(far_kernel, layout),
        out_shape=[jax.ShapeDtypeStruct((REACH, no, 2 * no), F32)] * count,
        in_specs=[SCALARS] + [WHOLE] * (len(tiles) + 2),
        out_specs=[WHOLE] * count,
        compiler_params=pltpu.CompilerParams(vmem_limit_bytes=VMEM_LIMIT),
        cost_estimate=FREE,
        name="far_part",
    )(odd, *tiles, weights, joined)


def crossed(real, imag):
    return jnp.concatenate(
        [jnp.concatenate([real, imag], axis=1), jnp.concatenate([-imag, real], axis=1)], axis=0
    )


def near_kernel(layouts, odd_ref, *refs):
    count = len(layouts[1])
    width, own_width = (len(layout) + sum(layout) for layout in layouts)
    tiles, refs = regroup(layouts[0], refs[:width]), refs[width:]
    owns, refs = regroup(layouts[1], refs[:own_width]), refs[own_width:]
    weights_ref, joined_ref = refs[:2]
    parts = refs[2 : 2 + count]
    out_real_ref, out_imag_ref = refs[-2:]
    no = joined_ref.shape[0]
    for c in range(count):

        @pl.when(pl.program_id(0) == c)
        def _():
            terms = hop_terms(odd_ref, tiles, c, weights_ref, joined_ref)
            sigmas = [(term + parts[c][i]).astype(BF16) for i, term in enumerate(terms)]
            greens = []
            for i in range(REACH):
                own = owns[c]
                green = jnp.where(odd_ref[0] > 0, own[0][i], own[1][i]) if isinstance(own, tuple) else own[i]
                greens.append((green[:no], green[no:]))
            prods = [
                dot(jnp.concatenate(pair, axis=1), crossed(sigma[:, :no], sigma[:, no:])).astype(BF16)
                for pair, sigma in zip(greens, sigmas)
            ]
            backs = [dot(prod, crossed(*pair)) / no for pair, prod in zip(greens, prods)]
            for i, ((real, imag), back) in enumerate(zip(greens, backs)):
                out_real_ref[0, i] = (real.astype(F32) + back[:, :no]).astype(BF16)
                out_imag_ref[0, i] = (imag.astype(F32) + back[:, no:]).astype(BF16)


def near_part(odd, tiles, weights, joined, owns, parts, start, shape, so_far):
    count = len(owns)
    layout, tiles = flat(tiles)
    own_layout, owns = flat(owns)
    no = joined.shape[0]
    block = pl.BlockSpec((1, REACH, no, no), lambda g: (0, start + g, 0, 0))
    shape = jax.ShapeDtypeStruct(shape, BF16)
    inputs = [odd, *tiles, *owns, weights, joined, *parts]
    in_specs = [SCALARS] + [WHOLE] * (len(inputs) - 1)
    aliases = {}
    if so_far is not None:
        aliases = {len(inputs): 0, len(inputs) + 1: 1}
        inputs += so_far
        in_specs += [UNTOUCHED] * 2
    return pl.pallas_call(
        functools.partial(near_kernel, (layout, own_layout)),
        grid=(count,),
        out_shape=(shape, shape),
        in_specs=in_specs,
        out_specs=(block, block),
        input_output_aliases=aliases,
        compiler_params=pltpu.CompilerParams(vmem_limit_bytes=VMEM_LIMIT),
        cost_estimate=FREE,
        name="near_part",
    )(*inputs)


def tied(x, *deps):
    return lax.optimization_barrier((x, *deps))[0] if deps else x


def shards(green_real, green_imag, coupling, strengths, offsets):
    chunks = green_real.shape[1] // REACH
    momenta, lanes = lax.axis_size("kz"), lax.axis_size("en")
    both = ("kz", "en")
    even = lax.axis_index("kz") % 2 == 0
    lane = lax.axis_index("en")
    odd_lane = lane % 2 == 1
    middle = lanes // 2
    at_middle = (lane == middle - 1) | (lane == middle)
    two_on = [(i, (i + 2) % momenta) for i in range(momenta)]
    swap = [(i, i ^ 1) for i in range(momenta)]
    outer = [p for m in range(1, lanes - 1, 2) for p in ((m, m + 1), (m + 1, m))]
    inner = [(i, i ^ 1) for i in range(lanes)]
    outer_turned = [
        (k * lanes + i, (k ^ 1 if {i, j} == {middle - 1, middle} else k) * lanes + j)
        for k in range(momenta)
        for i, j in outer
    ]

    def by_lane(odd, other):
        return jnp.where(odd_lane, odd, other)

    last = chunks - 1
    def cut(c, real, imag):
        energies = slice(c * REACH, (c + 1) * REACH)
        return jnp.concatenate([real[0, energies], imag[0, energies]], axis=1)

    green = (green_real, green_imag)
    own = [by_lane(cut(last, *green), cut(0, *green))]
    far, near = [lax.ppermute(own[0], "kz", two_on)], []
    green = lax.optimization_barrier((*green, own[0]))[:2]
    own.append(by_lane(cut(0, *green), cut(last, *green)))
    own += [cut(c, *green) for c in range(1, last)]
    for i in range(1, chunks):
        if i >= AHEAD:
            own[i] = tied(own[i], far[i - AHEAD])
        far.append(lax.ppermute(own[i], "kz", two_on))
    near_side, far_side = prepare(coupling, strengths, offsets)

    def arranged(sent, outer_halo, inner_halo):
        below, first = (inner_halo, outer_halo), (sent[1], sent[0])
        top, above = (sent[0], sent[1]), (outer_halo, inner_halo)
        return [below, first, *sent[2:], top, above]

    shape = green_real.shape
    odd = odd_lane.astype(jnp.int32).reshape(1)
    out, done = None, (far_side[0],)
    parts, halos, source = {}, {}, []
    far_work = {2: [0], 3: [1], 4: [2], 5: [3, 4, 5]}
    near_work = {4: [[0]], 5: [[1, 2]]}
    rest = [3, 4, 5]

    def grouped(sent, side, group):
        sent = sent + [sent[-1]] * (chunks - len(sent))
        return arranged(sent, halos[side, "outer"], halos[side, "inner"])[group[0] : group[-1] + 3]

    def after(tiles, done):
        tiles[-1] = tuple(tied(x, *done) for x in tiles[-1]) if isinstance(tiles[-1], tuple) else tied(tiles[-1], *done)
        return tiles

    for i in range(chunks):
        if i >= 2:
            done += (near[i - 2],)
        if i == 4:
            done += (halos["near", "outer"],)
        far[i] = tied(far[i], *done)
        source.append(jnp.where(even, own[i], far[i]))
        gate = [source[i]]
        if i == 0:
            halos["far", "outer"] = lax.ppermute(far[0], "en", outer)
        near.append(lax.ppermute(source[i], "kz", swap))
        if i == 1:
            halos["far", "inner"] = lax.ppermute(far[1], "en", inner)
        if i == 2:
            edge = tied(jnp.where(at_middle, source[0], near[0]), source[i])
            halos["near", "outer"] = lax.ppermute(edge, both, outer_turned)
            gate.append(edge)
        if i == 3:
            edge = tied(near[1], source[i])
            halos["near", "inner"] = lax.ppermute(edge, "en", inner)
            gate.append(edge)
        done = tuple(gate)
        if i in far_work:
            group = far_work[i]
            part = far_part(odd, after(grouped(far, "far", group), done), *far_side)
            for n, c in enumerate(group):
                parts[c] = part[n]
            done = (part[-1],)
        for group in near_work.get(i, []):
            owns = arranged(own, own[0], own[0])[group[0] + 1 : group[-1] + 2]
            tiles = grouped(near, "near", group)
            tiles[2] = tied(tiles[2], *done)
            out = near_part(odd, tiles, *near_side, owns, [parts[c] for c in group], group[0], shape, out)
            done = (out[0],)
    owns = arranged(own, own[0], own[0])[rest[0] + 1 : rest[-1] + 2]
    out = near_part(
        odd, grouped(near, "near", rest), *near_side, owns, [parts[c] for c in rest], rest[0], shape, out
    )
    return tuple(out)


def solution(mesh):
    in_specs = (
        P("kz", "en", None, None),
        P("kz", "en", None, None),
        P(None, None, "kz", None, None),
        P(),
        P(),
    )
    out_specs = (P("kz", "en", None, None), P("kz", "en", None, None))
    return jax.shard_map(shards, mesh=mesh, in_specs=in_specs, out_specs=out_specs, check_vma=False)
```

```python
import functools

import jax
import jax.numpy as jnp
from jax import lax
from jax.experimental import pallas as pl
from jax.experimental.pallas import tpu as pltpu
from jax.sharding import PartitionSpec as P

REACH = 4
HOPS = 2
BRANCHES = 4
WINDOW = 2 * REACH
AHEAD = 2
VMEM_LIMIT = 40 * 2**20

F32 = jnp.float32
BF16 = jnp.bfloat16
dot = functools.partial(jnp.dot, preferred_element_type=F32)
WHOLE = pl.BlockSpec(memory_space=pltpu.VMEM)
SCALARS = pl.BlockSpec(memory_space=pltpu.SMEM)
UNTOUCHED = pl.BlockSpec(memory_space=pl.ANY)
FREE = pl.CostEstimate(flops=0, bytes_accessed=10**6, transcendentals=0)


def prepare_kernel(s, offsets_ref, strengths_ref, coupling_ref, weights_ref, joined_ref):
    no = coupling_ref.shape[-1]
    for n in range(BRANCHES):
        matrix = coupling_ref[s, n, 0]
        joined_ref[:, n * no : (n + 1) * no] = matrix
        turned = matrix.astype(F32).T
        for i in range(WINDOW):
            w = offsets_ref[s, i]
            j = jnp.where(w > 0, REACH - w, REACH - 1 - w)
            rows = pl.ds(pl.multiple_of(j * no, no), no)
            weights_ref[rows, n * no : (n + 1) * no] = (strengths_ref[s, n, i] * turned).astype(BF16)


def prepare(s, coupling, strengths, offsets):
    no = coupling.shape[-1]
    return pl.pallas_call(
        functools.partial(prepare_kernel, s),
        out_shape=[
            jax.ShapeDtypeStruct((WINDOW * no, BRANCHES * no), BF16),
            jax.ShapeDtypeStruct((no, BRANCHES * no), BF16),
        ],
        in_specs=[SCALARS, SCALARS, WHOLE],
        out_specs=[WHOLE] * 2,
        compiler_params=pltpu.CompilerParams(vmem_limit_bytes=VMEM_LIMIT),
        cost_estimate=FREE,
        name="prepare",
    )(offsets, strengths, coupling)


def hop_terms(odd_ref, tiles, first, weights_ref, joined_ref):
    no = joined_ref.shape[0]

    def energy(t):
        tile = tiles[first + t // REACH]
        if isinstance(tile, tuple):
            return jnp.where(odd_ref[0] > 0, tile[0][t % REACH], tile[1][t % REACH])
        return tile[t % REACH]

    rows = []
    for i in range(REACH):
        rows.append(jnp.concatenate([energy(i + j + (j >= REACH)) for j in range(WINDOW)], axis=1))
    right = dot(jnp.concatenate(rows, axis=0), weights_ref[...]).astype(BF16)
    terms = []
    for i in range(REACH):
        stacked = []
        for n in range(BRANCHES):
            block = right[i * 2 * no : (i + 1) * 2 * no, n * no : (n + 1) * no]
            stacked.append(jnp.concatenate([block[:no], block[no:]], axis=1))
        terms.append(dot(joined_ref[...], jnp.concatenate(stacked, axis=0)))
    return terms


def regroup(layout, refs):
    refs = iter(refs)
    return [(next(refs), next(refs)) if pair else next(refs) for pair in layout]


def flat(tiles):
    layout = tuple(isinstance(tile, tuple) for tile in tiles)
    return layout, [x for tile in tiles for x in (tile if isinstance(tile, tuple) else (tile,))]


def far_kernel(layout, odd_ref, *refs):
    width = len(layout) + sum(layout)
    tiles, (weights_ref, joined_ref, *outs) = regroup(layout, refs[:width]), refs[width:]
    count = len(layout) - 2
    for c in range(count):
        for i, term in enumerate(hop_terms(odd_ref, tiles, c, weights_ref, joined_ref)):
            outs[c][i] = term


def far_part(odd, tiles, weights, joined):
    count = len(tiles) - 2
    layout, tiles = flat(tiles)
    no = joined.shape[0]
    return pl.pallas_call(
        functools.partial(far_kernel, layout),
        out_shape=[jax.ShapeDtypeStruct((REACH, no, 2 * no), F32)] * count,
        in_specs=[SCALARS] + [WHOLE] * (len(tiles) + 2),
        out_specs=[WHOLE] * count,
        compiler_params=pltpu.CompilerParams(vmem_limit_bytes=VMEM_LIMIT),
        cost_estimate=FREE,
        name="far_part",
    )(odd, *tiles, weights, joined)


def crossed(real, imag):
    return jnp.concatenate(
        [jnp.concatenate([real, imag], axis=1), jnp.concatenate([-imag, real], axis=1)], axis=0
    )


def near_kernel(layouts, odd_ref, *refs):
    count = len(layouts[1])
    width, own_width = (len(layout) + sum(layout) for layout in layouts)
    tiles, refs = regroup(layouts[0], refs[:width]), refs[width:]
    owns, refs = regroup(layouts[1], refs[:own_width]), refs[own_width:]
    weights_ref, joined_ref = refs[:2]
    parts = refs[2 : 2 + count]
    out_real_ref, out_imag_ref = refs[-2:]
    no = joined_ref.shape[0]
    for c in range(count):

        @pl.when(pl.program_id(0) == c)
        def _():
            terms = hop_terms(odd_ref, tiles, c, weights_ref, joined_ref)
            sigmas = [(term + parts[c][i]).astype(BF16) for i, term in enumerate(terms)]
            greens = []
            for i in range(REACH):
                own = owns[c]
                green = jnp.where(odd_ref[0] > 0, own[0][i], own[1][i]) if isinstance(own, tuple) else own[i]
                greens.append((green[:no], green[no:]))
            prods = [
                dot(jnp.concatenate(pair, axis=1), crossed(sigma[:, :no], sigma[:, no:])).astype(BF16)
                for pair, sigma in zip(greens, sigmas)
            ]
            backs = [dot(prod, crossed(*pair)) / no for pair, prod in zip(greens, prods)]
            for i, ((real, imag), back) in enumerate(zip(greens, backs)):
                out_real_ref[0, i] = (real.astype(F32) + back[:, :no]).astype(BF16)
                out_imag_ref[0, i] = (imag.astype(F32) + back[:, no:]).astype(BF16)


def near_part(odd, tiles, weights, joined, owns, parts, start, shape, so_far):
    count = len(owns)
    layout, tiles = flat(tiles)
    own_layout, owns = flat(owns)
    no = joined.shape[0]
    block = pl.BlockSpec((1, REACH, no, no), lambda g: (0, start + g, 0, 0))
    shape = jax.ShapeDtypeStruct(shape, BF16)
    inputs = [odd, *tiles, *owns, weights, joined, *parts]
    in_specs = [SCALARS] + [WHOLE] * (len(inputs) - 1)
    aliases = {}
    if so_far is not None:
        aliases = {len(inputs): 0, len(inputs) + 1: 1}
        inputs += so_far
        in_specs += [UNTOUCHED] * 2
    return pl.pallas_call(
        functools.partial(near_kernel, (layout, own_layout)),
        grid=(count,),
        out_shape=(shape, shape),
        in_specs=in_specs,
        out_specs=(block, block),
        input_output_aliases=aliases,
        compiler_params=pltpu.CompilerParams(vmem_limit_bytes=VMEM_LIMIT),
        cost_estimate=FREE,
        name="near_part",
    )(*inputs)


def tied(x, *deps):
    return lax.optimization_barrier((x, *deps))[0] if deps else x


def shards(green_real, green_imag, coupling, strengths, offsets):
    chunks = green_real.shape[1] // REACH
    momenta, lanes = lax.axis_size("kz"), lax.axis_size("en")
    both = ("kz", "en")
    even = lax.axis_index("kz") % 2 == 0
    lane = lax.axis_index("en")
    odd_lane = lane % 2 == 1
    middle = lanes // 2
    at_middle = (lane == middle - 1) | (lane == middle)
    two_on = [(i, (i + 2) % momenta) for i in range(momenta)]
    swap = [(i, i ^ 1) for i in range(momenta)]
    outer = [p for m in range(1, lanes - 1, 2) for p in ((m, m + 1), (m + 1, m))]
    inner = [(i, i ^ 1) for i in range(lanes)]
    outer_turned = [
        (k * lanes + i, (k ^ 1 if {i, j} == {middle - 1, middle} else k) * lanes + j)
        for k in range(momenta)
        for i, j in outer
    ]

    def by_lane(odd, other):
        return jnp.where(odd_lane, odd, other)

    last = chunks - 1
    def cut(c, real, imag):
        energies = slice(c * REACH, (c + 1) * REACH)
        return jnp.concatenate([real[0, energies], imag[0, energies]], axis=1)

    green = (green_real, green_imag)
    own = [by_lane(cut(last, *green), cut(0, *green))]
    far, near = [lax.ppermute(own[0], "kz", two_on)], []
    green = lax.optimization_barrier((*green, own[0]))[:2]
    own.append(by_lane(cut(0, *green), cut(last, *green)))
    own += [cut(c, *green) for c in range(1, last)]
    for i in range(1, chunks):
        if i >= AHEAD:
            own[i] = tied(own[i], far[i - AHEAD])
        far.append(lax.ppermute(own[i], "kz", two_on))
    near_side = prepare(0, coupling, strengths, offsets)

    def arranged(sent, outer_halo, inner_halo):
        below, first = (inner_halo, outer_halo), (sent[1], sent[0])
        top, above = (sent[0], sent[1]), (outer_halo, inner_halo)
        return [below, first, *sent[2:], top, above]

    shape = green_real.shape
    odd = odd_lane.astype(jnp.int32).reshape(1)
    out, done = None, (near_side[0],)
    parts, halos, source = {}, {}, []
    far_work = {2: [0], 3: [1], 4: [2], 5: [3, 4, 5]}
    near_work = {4: [[0]], 5: [[1, 2]]}
    rest = [3, 4, 5]

    def grouped(sent, side, group):
        sent = sent + [sent[-1]] * (chunks - len(sent))
        return arranged(sent, halos[side, "outer"], halos[side, "inner"])[group[0] : group[-1] + 3]

    def after(tiles, done):
        tiles[-1] = tuple(tied(x, *done) for x in tiles[-1]) if isinstance(tiles[-1], tuple) else tied(tiles[-1], *done)
        return tiles

    for i in range(chunks):
        if i >= 2:
            done += (near[i - 2],)
        if i == 4:
            done += (halos["near", "outer"],)
        far[i] = tied(far[i], *done)
        source.append(jnp.where(even, own[i], far[i]))
        gate = [source[i]]
        if i == 0:
            far_side = prepare(1, tied(coupling, source[0]), strengths, offsets)
            gate.append(far_side[0])
            halos["far", "outer"] = lax.ppermute(far[0], "en", outer)
        near.append(lax.ppermute(source[i], "kz", swap))
        if i == 1:
            halos["far", "inner"] = lax.ppermute(far[1], "en", inner)
        if i == 2:
            edge = tied(jnp.where(at_middle, source[0], near[0]), source[i])
            halos["near", "outer"] = lax.ppermute(edge, both, outer_turned)
            gate.append(edge)
        if i == 3:
            edge = tied(near[1], source[i])
            halos["near", "inner"] = lax.ppermute(edge, "en", inner)
            gate.append(edge)
        done = tuple(gate)
        if i in far_work:
            group = far_work[i]
            part = far_part(odd, after(grouped(far, "far", group), done), *far_side)
            for n, c in enumerate(group):
                parts[c] = part[n]
            done = (part[-1],)
        for group in near_work.get(i, []):
            owns = arranged(own, own[0], own[0])[group[0] + 1 : group[-1] + 2]
            tiles = grouped(near, "near", group)
            tiles[2] = tied(tiles[2], *done)
            out = near_part(odd, tiles, *near_side, owns, [parts[c] for c in group], group[0], shape, out)
            done = (out[0],)
    owns = arranged(own, own[0], own[0])[rest[0] + 1 : rest[-1] + 2]
    out = near_part(
        odd, grouped(near, "near", rest), *near_side, owns, [parts[c] for c in rest], rest[0], shape, out
    )
    return tuple(out)


def solution(mesh):
    in_specs = (
        P("kz", "en", None, None),
        P("kz", "en", None, None),
        P(None, None, "kz", None, None),
        P(),
        P(),
    )
    out_specs = (P("kz", "en", None, None), P("kz", "en", None, None))
    return jax.shard_map(shards, mesh=mesh, in_specs=in_specs, out_specs=out_specs, check_vma=False)
```

```python
import functools

import jax
import jax.numpy as jnp
from jax import lax
from jax.experimental import pallas as pl
from jax.experimental.pallas import tpu as pltpu
from jax.sharding import PartitionSpec as P

REACH = 4
HOPS = 2
BRANCHES = 4
WINDOW = 2 * REACH
AHEAD = 2
VMEM_LIMIT = 40 * 2**20

F32 = jnp.float32
BF16 = jnp.bfloat16
dot = functools.partial(jnp.dot, preferred_element_type=F32)
WHOLE = pl.BlockSpec(memory_space=pltpu.VMEM)
SCALARS = pl.BlockSpec(memory_space=pltpu.SMEM)
UNTOUCHED = pl.BlockSpec(memory_space=pl.ANY)
FREE = pl.CostEstimate(flops=0, bytes_accessed=10**6, transcendentals=0)


def prepare_kernel(s, offsets_ref, strengths_ref, coupling_ref, weights_ref, joined_ref):
    no = coupling_ref.shape[-1]
    for n in range(BRANCHES):
        matrix = coupling_ref[s, n, 0]
        joined_ref[:, n * no : (n + 1) * no] = matrix
        turned = matrix.astype(F32).T
        for i in range(WINDOW):
            w = offsets_ref[s, i]
            j = jnp.where(w > 0, REACH - w, REACH - 1 - w)
            rows = pl.ds(pl.multiple_of(j * no, no), no)
            weights_ref[rows, n * no : (n + 1) * no] = (strengths_ref[s, n, i] * turned).astype(BF16)


def prepare(s, coupling, strengths, offsets):
    no = coupling.shape[-1]
    return pl.pallas_call(
        functools.partial(prepare_kernel, s),
        out_shape=[
            jax.ShapeDtypeStruct((WINDOW * no, BRANCHES * no), BF16),
            jax.ShapeDtypeStruct((no, BRANCHES * no), BF16),
        ],
        in_specs=[SCALARS, SCALARS, WHOLE],
        out_specs=[WHOLE] * 2,
        compiler_params=pltpu.CompilerParams(vmem_limit_bytes=VMEM_LIMIT),
        cost_estimate=FREE,
        name="prepare",
    )(offsets, strengths, coupling)


def hop_terms(odd_ref, tiles, first, weights_ref, joined_ref):
    no = joined_ref.shape[0]

    def energy(t):
        tile = tiles[first + t // REACH]
        if isinstance(tile, tuple):
            return jnp.where(odd_ref[0] > 0, tile[0][t % REACH], tile[1][t % REACH])
        return tile[t % REACH]

    rows = []
    for i in range(REACH):
        rows.append(jnp.concatenate([energy(i + j + (j >= REACH)) for j in range(WINDOW)], axis=1))
    right = dot(jnp.concatenate(rows, axis=0), weights_ref[...]).astype(BF16)
    terms = []
    for i in range(REACH):
        stacked = []
        for n in range(BRANCHES):
            block = right[i * 2 * no : (i + 1) * 2 * no, n * no : (n + 1) * no]
            stacked.append(jnp.concatenate([block[:no], block[no:]], axis=1))
        terms.append(dot(joined_ref[...], jnp.concatenate(stacked, axis=0)))
    return terms


def regroup(layout, refs):
    refs = iter(refs)
    return [(next(refs), next(refs)) if pair else next(refs) for pair in layout]


def flat(tiles):
    layout = tuple(isinstance(tile, tuple) for tile in tiles)
    return layout, [x for tile in tiles for x in (tile if isinstance(tile, tuple) else (tile,))]


def far_kernel(layout, odd_ref, *refs):
    width = len(layout) + sum(layout)
    tiles, (weights_ref, joined_ref, *outs) = regroup(layout, refs[:width]), refs[width:]
    count = len(layout) - 2
    for c in range(count):
        for i, term in enumerate(hop_terms(odd_ref, tiles, c, weights_ref, joined_ref)):
            outs[c][i] = term


def far_part(odd, tiles, weights, joined):
    count = len(tiles) - 2
    layout, tiles = flat(tiles)
    no = joined.shape[0]
    return pl.pallas_call(
        functools.partial(far_kernel, layout),
        out_shape=[jax.ShapeDtypeStruct((REACH, no, 2 * no), F32)] * count,
        in_specs=[SCALARS] + [WHOLE] * (len(tiles) + 2),
        out_specs=[WHOLE] * count,
        compiler_params=pltpu.CompilerParams(vmem_limit_bytes=VMEM_LIMIT),
        cost_estimate=FREE,
        name="far_part",
    )(odd, *tiles, weights, joined)


def crossed(real, imag):
    return jnp.concatenate(
        [jnp.concatenate([real, imag], axis=1), jnp.concatenate([-imag, real], axis=1)], axis=0
    )


def near_kernel(layouts, odd_ref, *refs):
    count = len(layouts[1])
    width, own_width = (len(layout) + sum(layout) for layout in layouts)
    tiles, refs = regroup(layouts[0], refs[:width]), refs[width:]
    owns, refs = regroup(layouts[1], refs[:own_width]), refs[own_width:]
    weights_ref, joined_ref = refs[:2]
    parts = refs[2 : 2 + count]
    out_real_ref, out_imag_ref = refs[-2:]
    no = joined_ref.shape[0]
    for c in range(count):

        @pl.when(pl.program_id(0) == c)
        def _():
            terms = hop_terms(odd_ref, tiles, c, weights_ref, joined_ref)
            sigmas = [(term + parts[c][i]).astype(BF16) for i, term in enumerate(terms)]
            greens = []
            for i in range(REACH):
                own = owns[c]
                green = jnp.where(odd_ref[0] > 0, own[0][i], own[1][i]) if isinstance(own, tuple) else own[i]
                greens.append((green[:no], green[no:]))
            prods = [
                dot(jnp.concatenate(pair, axis=1), crossed(sigma[:, :no], sigma[:, no:])).astype(BF16)
                for pair, sigma in zip(greens, sigmas)
            ]
            backs = [dot(prod, crossed(*pair)) / no for pair, prod in zip(greens, prods)]
            for i, ((real, imag), back) in enumerate(zip(greens, backs)):
                out_real_ref[0, i] = (real.astype(F32) + back[:, :no]).astype(BF16)
                out_imag_ref[0, i] = (imag.astype(F32) + back[:, no:]).astype(BF16)


def near_part(odd, tiles, weights, joined, owns, parts, start, shape, so_far):
    count = len(owns)
    layout, tiles = flat(tiles)
    own_layout, owns = flat(owns)
    no = joined.shape[0]
    block = pl.BlockSpec((1, REACH, no, no), lambda g: (0, start + g, 0, 0))
    shape = jax.ShapeDtypeStruct(shape, BF16)
    inputs = [odd, *tiles, *owns, weights, joined, *parts]
    in_specs = [SCALARS] + [WHOLE] * (len(inputs) - 1)
    aliases = {}
    if so_far is not None:
        aliases = {len(inputs): 0, len(inputs) + 1: 1}
        inputs += so_far
        in_specs += [UNTOUCHED] * 2
    return pl.pallas_call(
        functools.partial(near_kernel, (layout, own_layout)),
        grid=(count,),
        out_shape=(shape, shape),
        in_specs=in_specs,
        out_specs=(block, block),
        input_output_aliases=aliases,
        compiler_params=pltpu.CompilerParams(vmem_limit_bytes=VMEM_LIMIT),
        cost_estimate=FREE,
        name="near_part",
    )(*inputs)


def tied(x, *deps):
    return lax.optimization_barrier((x, *deps))[0] if deps else x


def shards(green_real, green_imag, coupling, strengths, offsets):
    chunks = green_real.shape[1] // REACH
    momenta, lanes = lax.axis_size("kz"), lax.axis_size("en")
    both = ("kz", "en")
    even = lax.axis_index("kz") % 2 == 0
    lane = lax.axis_index("en")
    odd_lane = lane % 2 == 1
    middle = lanes // 2
    at_middle = (lane == middle - 1) | (lane == middle)
    two_on = [(i, (i + 2) % momenta) for i in range(momenta)]
    swap = [(i, i ^ 1) for i in range(momenta)]
    outer = [p for m in range(1, lanes - 1, 2) for p in ((m, m + 1), (m + 1, m))]
    inner = [(i, i ^ 1) for i in range(lanes)]
    outer_turned = [
        (k * lanes + i, (k ^ 1 if {i, j} == {middle - 1, middle} else k) * lanes + j)
        for k in range(momenta)
        for i, j in outer
    ]

    def by_lane(odd, other):
        return jnp.where(odd_lane, odd, other)

    last = chunks - 1
    def cut(c, real, imag):
        energies = slice(c * REACH, (c + 1) * REACH)
        return jnp.concatenate([real[0, energies], imag[0, energies]], axis=1)

    green = (green_real, green_imag)
    own = [by_lane(cut(last, *green), cut(0, *green))]
    far, near = [lax.ppermute(own[0], "kz", two_on)], []
    green = lax.optimization_barrier((*green, own[0]))[:2]
    own.append(by_lane(cut(0, *green), cut(last, *green)))
    own += [cut(c, *green) for c in range(1, last)]
    for i in range(1, chunks):
        if i >= AHEAD:
            own[i] = tied(own[i], far[i - AHEAD])
        far.append(lax.ppermute(own[i], "kz", two_on))
    near_side = prepare(0, coupling, strengths, offsets)

    def arranged(sent, outer_halo, inner_halo):
        below, first = (inner_halo, outer_halo), (sent[1], sent[0])
        top, above = (sent[0], sent[1]), (outer_halo, inner_halo)
        return [below, first, *sent[2:], top, above]

    shape = green_real.shape
    odd = odd_lane.astype(jnp.int32).reshape(1)
    out, done = None, (near_side[0],)
    parts, halos, source = {}, {}, []
    far_work = {3: [1], 4: [0], 5: [2, 3, 4, 5]}
    near_work = {4: [[0, 1]], 5: [[2]]}
    rest = [3, 4, 5]

    def grouped(sent, side, group):
        sent = sent + [sent[-1]] * (chunks - len(sent))
        return arranged(sent, halos[side, "outer"], halos[side, "inner"])[group[0] : group[-1] + 3]

    def after(tiles, done):
        tiles[-1] = tuple(tied(x, *done) for x in tiles[-1]) if isinstance(tiles[-1], tuple) else tied(tiles[-1], *done)
        return tiles

    for i in range(chunks):
        if i >= 2:
            done += (near[i - 2],)
        if i == 4:
            done += (halos["near", "outer"],)
        far[i] = tied(far[i], *done)
        source.append(jnp.where(even, own[i], far[i]))
        gate = [source[i]]
        if i == 0:
            far_side = prepare(1, tied(coupling, source[0]), strengths, offsets)
            gate.append(far_side[0])
            halos["far", "outer"] = lax.ppermute(far[0], "en", outer)
        near.append(lax.ppermute(source[i], "kz", swap))
        if i == 1:
            halos["far", "inner"] = lax.ppermute(far[1], "en", inner)
        if i == 2:
            edge = tied(jnp.where(at_middle, source[0], near[0]), source[i])
            halos["near", "outer"] = lax.ppermute(edge, both, outer_turned)
            gate.append(edge)
        if i == 3:
            edge = tied(near[1], source[i])
            halos["near", "inner"] = lax.ppermute(edge, "en", inner)
            gate.append(edge)
        done = tuple(gate)
        if i in far_work:
            group = far_work[i]
            part = far_part(odd, after(grouped(far, "far", group), done), *far_side)
            for n, c in enumerate(group):
                parts[c] = part[n]
            done = (part[-1],)
        for group in near_work.get(i, []):
            owns = arranged(own, own[0], own[0])[group[0] + 1 : group[-1] + 2]
            tiles = grouped(near, "near", group)
            tiles[2] = tied(tiles[2], *done)
            out = near_part(odd, tiles, *near_side, owns, [parts[c] for c in group], group[0], shape, out)
            done = (out[0],)
    owns = arranged(own, own[0], own[0])[rest[0] + 1 : rest[-1] + 2]
    out = near_part(
        odd, grouped(near, "near", rest), *near_side, owns, [parts[c] for c in rest], rest[0], shape, out
    )
    return tuple(out)


def solution(mesh):
    in_specs = (
        P("kz", "en", None, None),
        P("kz", "en", None, None),
        P(None, None, "kz", None, None),
        P(),
        P(),
    )
    out_specs = (P("kz", "en", None, None), P("kz", "en", None, None))
    return jax.shard_map(shards, mesh=mesh, in_specs=in_specs, out_specs=out_specs, check_vma=False)
```
